32 devices in a mesh: grp: 2 (over y), gx: 4 (over x, core), gy: 4 (over z).
Axes of the slice: x: 2, y: 2, z: 4, core: 2. Of those that a mesh axis runs over, the one named last changes fastest.
Arguments:
- hidden: bfloat16 [1088, 8, 3200], P('gy', 'grp', 'gx'), parts along dimension 1, may hold values from -6 to 6
- qkv: bfloat16 [1088, 8, 6144], P('gy', 'grp', 'gx'), parts along dimension 1, may hold values from -10 to 10
- w_qkv: bfloat16 [3200, 6144], P('gy', 'gx'), may hold values from -0.109375 to 0.109375
- w_out: bfloat16 [3200, 2048], P('gy', 'gx'), may hold values from -0.109375 to 0.109375
- grad_out: bfloat16 [1088, 8, 3200], P('gy', 'grp', 'gx'), parts along dimension 1, may hold values from -6 to 6
- lengths: int32 [8], P('grp'), parts along dimension 0, may hold values from 544 to 1088, as said below
Outputs:
- grad_hidden: bfloat16 [1088, 8, 3200], P('gy', 'grp', 'gx'), parts along dimension 1
- grad_w_qkv: float32 [6400, 6144], P(('grp', 'gy'), 'gx'), parts along dimension 0
- grad_w_out: float32 [6400, 2048], P(('grp', 'gy'), 'gx'), parts along dimension 0
The draws below stay inside these ranges and needn't reach their ends.
There are 2 independent parts, one for each index of `grp`. The reference program is written for one: setup_inputs(seed, part) draws one part's arguments, and reference() takes and returns one part's arrays. A program takes and returns all parts, laid end to end along the dimension named above; an argument that names none is the same for every part. Nothing has to cross between parts.
Inputs may be any that keep to these rules, and one draw needn't show every extreme that they name: Keys at positions lengths[b] and beyond are masked for image b; exactly one image has all 1088 slots valid.
All inputs are finite; a program needn't handle non-finite values.
Results may differ from the reference program's by a relative error of at most 0.017.
Values may be sent and summed in bfloat16 or wider, within the bound.
A program may use at most 256 MiB of HBM per device.

```python
import math
import jax
import jax.numpy as jnp
from jax import lax

D = 3200
HEAD_DIM = 128
HEADS = 16
SEQ = 1088
IMGS = 4


def draw_lengths(key, part):
    key = jax.random.fold_in(key, 11)
    first_key, second_key = jax.random.split(key)
    counts = jax.random.randint(first_key, (IMGS,), SEQ // 2, SEQ)
    full_image = jax.random.randint(second_key, (), 0, IMGS)
    return jnp.where(jnp.arange(IMGS) == full_image, SEQ, counts).astype(jnp.int32)


def draw_qkv(key, part):
    key = jax.random.fold_in(key, 23)
    key_list = jax.random.split(key, 1)
    shape = (SEQ, IMGS, HEADS, 3, HEAD_DIM)
    base = jnp.clip(1.4 * jax.random.normal(key_list[0], shape, jnp.float32), -8.0, 8.0)
    return base.reshape(SEQ, IMGS, 3 * HEADS * HEAD_DIM).astype(jnp.bfloat16)


def block_scale(key, extent, pieces, least, high):
    def one(position, blocks):
        draws = jax.random.uniform(jax.random.fold_in(jax.random.fold_in(key, 6), position), (blocks,), jnp.float32, least / len(pieces), high / len(pieces))
        return jnp.repeat(jnp.exp(draws), extent[position] // blocks).reshape((-1,) + (1,) * (len(extent) - position - 1))

    level = one(*pieces[0])
    for cut in pieces[1:]:
        level = level * one(*cut)
    return level


def normal_values(own_key, dims, spread, limit, cuts=(), kind=jnp.bfloat16):
    values = jax.random.normal(own_key, dims, jnp.float32) * spread
    if len(cuts) > 0:
        values = block_scale(own_key, dims, cuts, -0.22, 0.18) * values
    return jnp.clip(values, min=-limit, max=limit).astype(kind)


def setup_inputs(seed: int = 0, part: int = 0) -> dict:
    streams_of = jax.random.split(jax.random.key(seed), 7)
    own_keys = jax.random.split(jax.random.fold_in(streams_of[6], part), 7)
    hidden = normal_values(own_keys[0], (SEQ, IMGS, D), 1.0, 6.0, ((0, 4), (2, 4)))
    qkv = draw_qkv(jax.random.fold_in(jax.random.fold_in(streams_of[6], part), 71), part)
    w_qkv = normal_values(streams_of[2], (D, 3 * HEADS * HEAD_DIM), D ** -0.5, 0.109375, ((0, 4), (1, 4)))
    w_out = normal_values(streams_of[3], (D, HEADS * HEAD_DIM), D ** -0.5, 0.109375, ((0, 4), (1, 4)))
    grad_out = normal_values(own_keys[4], (SEQ, IMGS, D), 1.0, 6.0, ((0, 4), (2, 4)))
    lengths = draw_lengths(jax.random.fold_in(jax.random.fold_in(streams_of[6], part), 71), part)
    return dict(hidden=hidden, qkv=qkv, w_qkv=w_qkv, w_out=w_out, grad_out=grad_out, lengths=lengths)


def head_backward(query_rows, key_rows, value_rows, grad_head, valid_keys):
    score_scale = 1.0 / math.sqrt(HEAD_DIM)
    query_f = query_rows.astype(jnp.float32)
    key_f = key_rows.astype(jnp.float32)
    value_f = value_rows.astype(jnp.float32)
    grad_f = grad_head.astype(jnp.float32)
    scores = jnp.einsum('bse,bte->bst', query_f, key_f) * score_scale
    valid_grid = valid_keys[:, None, :]
    masked = jnp.where(valid_grid, scores, -jnp.inf)
    row_max = lax.optimization_barrier(jnp.max(masked, axis=2, keepdims=True))
    row_total = lax.optimization_barrier(jnp.sum(jnp.where(valid_grid, jnp.exp(scores - row_max), 0.0), axis=2, keepdims=True))
    log_total = row_max + jnp.log(row_total)
    probs_full = jnp.where(valid_grid, jnp.exp(scores - log_total), 0.0)
    probs_low = probs_full.astype(jnp.bfloat16)
    probs_back = probs_low.astype(jnp.float32)
    attn_out = jnp.einsum('bst,bte->bse', probs_back, value_f).astype(jnp.bfloat16)
    row_dots = lax.optimization_barrier(jnp.sum(grad_f * attn_out.astype(jnp.float32), axis=2, keepdims=True))
    grad_prob = jnp.einsum('bse,bte->bst', grad_f, value_f)
    grad_score = (probs_full * (grad_prob - row_dots) * score_scale).astype(jnp.bfloat16)
    score_back = grad_score.astype(jnp.float32)
    grad_q = jnp.einsum('bst,bte->bse', score_back, key_f).astype(jnp.bfloat16)
    grad_k = jnp.einsum('bst,bse->bte', score_back, query_f).astype(jnp.bfloat16)
    grad_v = jnp.einsum('bst,bse->bte', probs_back, grad_f).astype(jnp.bfloat16)
    return (attn_out, grad_q, grad_k, grad_v)

def reference(hidden, qkv, w_qkv, w_out, grad_out, lengths):
    row_count = SEQ * IMGS
    grad_rows = grad_out.reshape(row_count, D)
    grad_attn = jnp.dot(grad_rows, w_out, preferred_element_type=jnp.float32).astype(jnp.bfloat16)
    grad_heads = grad_attn.reshape(SEQ, IMGS, HEADS, HEAD_DIM).transpose(2, 1, 0, 3)
    head_parts = qkv.reshape(SEQ, IMGS, HEADS, 3, HEAD_DIM).transpose(2, 3, 1, 0, 4)
    valid_keys = jnp.arange(SEQ)[None, :] < lengths[:, None]

    def one_head(inputs):
        head_part, grad_head = inputs
        return head_backward(head_part[0], head_part[1], head_part[2], grad_head, valid_keys)
    attn_out, grad_q, grad_k, grad_v = lax.map(one_head, (head_parts, grad_heads))
    attn_rows = attn_out.transpose(2, 1, 0, 3).reshape(row_count, HEADS * HEAD_DIM)
    stacked = jnp.stack([grad_q, grad_k, grad_v], axis=1)
    grad_qkv = stacked.transpose(3, 2, 0, 1, 4).reshape(row_count, 3 * HEADS * HEAD_DIM)
    grad_hidden = jnp.dot(grad_qkv, w_qkv.T, preferred_element_type=jnp.float32).astype(jnp.bfloat16)
    grad_hidden = grad_hidden.reshape(SEQ, IMGS, D)
    hidden_rows = hidden.reshape(row_count, D)
    grad_w_qkv = jnp.dot(hidden_rows.T, grad_qkv, preferred_element_type=jnp.float32)
    grad_w_out = jnp.dot(grad_rows.T, attn_rows, preferred_element_type=jnp.float32)
    return (grad_hidden, grad_w_qkv, grad_w_out)
```

```python
import functools
import math

import jax
import jax.numpy as jnp
from jax import lax
from jax.experimental import pallas as pl
from jax.experimental.pallas import tpu as pltpu
from jax.sharding import PartitionSpec as P

D = 3200
HEAD_DIM = 128


def contract_rows(left_rows, right_rows):
    return lax.dot_general(
        left_rows, right_rows, (((0,), (0,)), ((), ())), preferred_element_type=jnp.float32
    )


def softmax_totals(scores, valid_grid):
    masked = jnp.where(valid_grid, scores, -jnp.inf)
    row_max = jnp.max(masked, axis=3, keepdims=True)
    row_total = jnp.sum(
        jnp.where(valid_grid, jnp.exp(scores - row_max), 0.0), axis=3, keepdims=True
    )
    return row_max + jnp.log(row_total)


def shards(hidden, qkv, w_qkv, w_out, grad_out, lengths):
    seq_dev, image_count, column_count = qkv.shape
    heads_dev = column_count // (3 * HEAD_DIM)
    score_scale = 1.0 / math.sqrt(HEAD_DIM)
    row_count = seq_dev * image_count
    qkv_parts = qkv.reshape(seq_dev, image_count, heads_dev, 3, HEAD_DIM)
    query_rows = qkv_parts[:, :, :, 0]
    key_values = qkv_parts[:, :, :, 1:].reshape(seq_dev, image_count, heads_dev * 2 * HEAD_DIM)
    grad_full, hidden_full = (
        lax.all_gather(grad_out, "gx", axis=2, tiled=True),
        lax.all_gather(hidden, "gx", axis=2, tiled=True),
    )
    w_qkv_full, w_out_full, kv_full = (
        lax.all_gather(w_qkv, "gy", axis=0, tiled=True),
        lax.all_gather(w_out, "gy", axis=0, tiled=True),
        lax.all_gather(key_values, "gy", axis=0, tiled=True),
    )
    grad_rows = grad_full.reshape(row_count, D)
    grad_attn = jnp.dot(grad_rows, w_out_full, preferred_element_type=jnp.float32).astype(
        jnp.bfloat16
    )
    grad_attn = grad_attn.reshape(seq_dev, image_count, heads_dev, HEAD_DIM)
    seq_total = kv_full.shape[0]
    kv_parts = kv_full.reshape(seq_total, image_count, heads_dev, 2, HEAD_DIM)
    key_all = kv_parts[:, :, :, 0]
    value_all = kv_parts[:, :, :, 1]
    valid_all = (jnp.arange(seq_total)[None, :] < lengths[:, None])[:, None, None, :]
    scores = (
        jnp.einsum("sbhe,tbhe->bhst", query_rows, key_all, preferred_element_type=jnp.float32)
        * score_scale
    )
    log_total = softmax_totals(scores, valid_all)
    probs_full = jnp.where(valid_all, jnp.exp(scores - log_total), 0.0)
    probs_low = probs_full.astype(jnp.bfloat16)
    attn_out = jnp.einsum(
        "bhst,tbhe->sbhe", probs_low, value_all, preferred_element_type=jnp.float32
    ).astype(jnp.bfloat16)
    row_dots = jnp.sum(grad_attn.astype(jnp.float32) * attn_out.astype(jnp.float32), axis=3)
    dots_grid = row_dots.transpose(1, 2, 0)[..., None]
    grad_prob = jnp.einsum(
        "sbhe,tbhe->bhst", grad_attn, value_all, preferred_element_type=jnp.float32
    )
    grad_score = (probs_full * (grad_prob - dots_grid) * score_scale).astype(jnp.bfloat16)
    grad_q = jnp.einsum(
        "bhst,tbhe->sbhe", grad_score, key_all, preferred_element_type=jnp.float32
    ).astype(jnp.bfloat16)
    key_terms = jnp.einsum(
        "bhst,sbhe->tbhe", grad_score, query_rows, preferred_element_type=jnp.float32
    )
    value_terms = jnp.einsum(
        "bhst,sbhe->tbhe", probs_low, grad_attn, preferred_element_type=jnp.float32
    )
    kv_terms = jnp.stack([key_terms, value_terms], axis=3).reshape(
        seq_total, image_count, heads_dev * 2 * HEAD_DIM
    )
    summed = lax.psum_scatter(kv_terms, "gy", scatter_dimension=0, tiled=True)
    grad_kv = summed.astype(jnp.bfloat16).reshape(seq_dev, image_count, heads_dev, 2, HEAD_DIM)
    grad_qkv = jnp.concatenate([grad_q[:, :, :, None], grad_kv], axis=3).reshape(
        seq_dev, image_count, column_count
    )
    grad_qkv_rows = grad_qkv.reshape(row_count, column_count)
    hidden_terms = lax.dot_general(
        grad_qkv_rows, w_qkv_full, (((1,), (1,)), ((), ())), preferred_element_type=jnp.float32
    )
    grad_hidden = lax.psum_scatter(
        hidden_terms.reshape(seq_dev, image_count, D), "gx", scatter_dimension=2, tiled=True
    ).astype(jnp.bfloat16)
    attn_rows = attn_out.reshape(row_count, heads_dev * HEAD_DIM)
    out_terms = contract_rows(grad_rows, attn_rows)
    qkv_terms = contract_rows(hidden_full.reshape(row_count, D), grad_qkv_rows)
    grad_w_qkv, grad_w_out = (
        lax.psum_scatter(qkv_terms, "gy", scatter_dimension=0, tiled=True),
        lax.psum_scatter(out_terms, "gy", scatter_dimension=0, tiled=True),
    )
    return (grad_hidden, grad_w_qkv, grad_w_out)


def dot(left, right, dims):
    return lax.dot_general(left, right, ((dims[0], dims[1]), ((), ())), preferred_element_type=jnp.float32)


def head_kernel(block, length_ref, qkv_ref, grad_ref, attn_ref, dqkv_ref, key_sum, value_sum):
    seq = qkv_ref.shape[0]
    score_scale = 1.0 / math.sqrt(HEAD_DIM)
    length = length_ref[0]
    key_sum[...] = jnp.zeros_like(key_sum)
    value_sum[...] = jnp.zeros_like(value_sum)

    @pl.loop(0, seq // block)
    def _(step):
        rows = pl.ds(pl.multiple_of(step * block, block), block)
        q = qkv_ref[rows, 0:HEAD_DIM]
        k = qkv_ref[:, HEAD_DIM : 2 * HEAD_DIM]
        v = qkv_ref[:, 2 * HEAD_DIM :]
        g = grad_ref[rows, :]
        valid = lax.broadcasted_iota(jnp.int32, (1, seq), 1) < length
        scores = dot(q, k, ((1,), (1,))) * score_scale
        masked = jnp.where(valid, scores, -jnp.inf)
        row_max = jnp.max(masked, axis=1, keepdims=True)
        terms = jnp.exp(masked - row_max)
        probs = terms * (1.0 / jnp.sum(terms, axis=1, keepdims=True))
        probs_low = probs.astype(jnp.bfloat16)
        attn = dot(probs_low, v, ((1,), (0,))).astype(jnp.bfloat16)
        attn_ref[rows, :] = attn
        row_dots = jnp.sum(g.astype(jnp.float32) * attn.astype(jnp.float32), axis=1, keepdims=True)
        grad_prob = dot(g, v, ((1,), (1,)))
        grad_score = (probs * ((grad_prob - row_dots) * score_scale)).astype(jnp.bfloat16)
        dqkv_ref[rows, 0:HEAD_DIM] = dot(grad_score, k, ((1,), (0,))).astype(jnp.bfloat16)
        key_sum[...] += dot(grad_score, q, ((0,), (0,)))
        value_sum[...] += dot(probs_low, g, ((0,), (0,)))

    dqkv_ref[:, HEAD_DIM : 2 * HEAD_DIM] = key_sum[...].astype(jnp.bfloat16)
    dqkv_ref[:, 2 * HEAD_DIM :] = value_sum[...].astype(jnp.bfloat16)


def attention_backward(length, qkv, grad_attn):
    seq = qkv.shape[0]
    heads = qkv.shape[1] // (3 * HEAD_DIM)
    block = 272 if seq % 272 == 0 else seq
    return pl.pallas_call(
        functools.partial(head_kernel, block),
        grid=(heads,),
        in_specs=[
            pl.BlockSpec(memory_space=pltpu.SMEM),
            pl.BlockSpec((seq, 3 * HEAD_DIM), lambda h: (0, h)),
            pl.BlockSpec((seq, HEAD_DIM), lambda h: (0, h)),
        ],
        out_specs=[
            pl.BlockSpec((seq, HEAD_DIM), lambda h: (0, h)),
            pl.BlockSpec((seq, 3 * HEAD_DIM), lambda h: (0, h)),
        ],
        out_shape=[
            jax.ShapeDtypeStruct((seq, heads * HEAD_DIM), jnp.bfloat16),
            jax.ShapeDtypeStruct((seq, heads * 3 * HEAD_DIM), jnp.bfloat16),
        ],
        scratch_shapes=[
            pltpu.VMEM((seq, HEAD_DIM), jnp.float32),
            pltpu.VMEM((seq, HEAD_DIM), jnp.float32),
        ],
        compiler_params=pltpu.CompilerParams(vmem_limit_bytes=40 * 2**20),
        cost_estimate=pl.CostEstimate(
            flops=14 * heads * seq * seq * HEAD_DIM,
            bytes_accessed=16 * heads * seq * HEAD_DIM,
            transcendentals=heads * seq * seq,
        ),
    )(length, qkv, grad_attn)


def by_image(rows):
    swapped = lax.all_to_all(rows.transpose(1, 0, 2), "gy", 0, 0)
    return swapped.reshape(-1, rows.shape[2])


def weight_rows(weight):
    half = weight.shape[0] // 2
    group, me = lax.axis_index("grp"), lax.axis_index("gy")
    share = lax.dynamic_slice_in_dim(weight, group * half, half, 0)
    mine = lax.all_gather(share, "gy")
    full = jnp.zeros((4, 2) + share.shape, weight.dtype)
    full = lax.dynamic_update_slice(full, weight.reshape((1, 2) + share.shape), (me, 0, 0, 0))
    for bits in (1, 2, 3):
        part = lax.dynamic_slice_in_dim(mine, me ^ bits, 1, 0)
        other = lax.ppermute(part, "grp", [(0, 1), (1, 0)])
        full = lax.dynamic_update_slice(full, part[None], (me ^ bits, group, 0, 0))
        full = lax.dynamic_update_slice(full, other[None], (me ^ bits, 1 - group, 0, 0))
    return full.reshape((4,) + weight.shape)


def spread_images(rows):
    me = lax.axis_index("gy")
    blocks = rows.transpose(1, 0, 2)
    full = jnp.zeros(blocks.shape, blocks.dtype)
    for bits in range(4):
        part = lax.dynamic_index_in_dim(blocks, me ^ bits, 0, keepdims=False)
        if bits:
            part = lax.ppermute(part, "gy", [(i, i ^ bits) for i in range(4)])
        full = lax.dynamic_update_index_in_dim(full, part, me ^ bits, 0)
    return full.reshape(-1, rows.shape[2])


def flip(value, bits):
    return lax.ppermute(value, "gx", [(i, i ^ bits) for i in range(4)])


def feature_blocks(own):
    across = flip(own, 2)
    beside = flip(own, 1)
    corner = flip(across, 1)
    me = lax.axis_index("gx")
    full = jnp.zeros((4,) + own.shape, own.dtype)
    for bits, part in enumerate((own, beside, across, corner)):
        full = lax.dynamic_update_index_in_dim(full, part, me ^ bits, 0)
    return full


def sum_features(terms):
    me = lax.axis_index("gx")

    def block(bits):
        return lax.dynamic_index_in_dim(terms, me ^ bits, 0, keepdims=False)

    far = block(2).astype(jnp.float32) + flip(block(3), 1).astype(jnp.float32)
    near = block(0).astype(jnp.float32) + flip(block(1), 1).astype(jnp.float32)
    return (near + flip(far.astype(jnp.bfloat16), 2).astype(jnp.float32)).astype(jnp.bfloat16)


def image_shards(gy_count, hidden, qkv, w_qkv, w_out, grad_out, lengths):
    image = lax.axis_index("gy")
    length = lax.dynamic_slice(lengths, (image,), (1,))
    seq_dev = qkv.shape[0]
    w_out_full = weight_rows(w_out)
    grad_own = by_image(grad_out)
    grad_rows = feature_blocks(grad_own)
    qkv, grad_own = lax.optimization_barrier((qkv, grad_own))
    qkv_rows = spread_images(qkv)
    hidden, qkv_rows = lax.optimization_barrier((hidden, qkv_rows))
    w_qkv, grad_own = lax.optimization_barrier((w_qkv, grad_own))
    w_qkv_full = weight_rows(w_qkv)
    hidden_rows = feature_blocks(spread_images(hidden))
    w_qkv_full, hidden_rows = lax.optimization_barrier((w_qkv_full, hidden_rows))
    grad_attn = jnp.einsum(
        "ird,idc->rc", grad_rows, w_out_full, preferred_element_type=jnp.float32
    ).astype(jnp.bfloat16)
    attn_out, grad_qkv = attention_backward(length, qkv_rows, grad_attn)
    out_terms = jnp.einsum("ird,rc->idc", grad_rows, attn_out, preferred_element_type=jnp.float32)
    grad_w_out = lax.psum_scatter(out_terms.astype(jnp.bfloat16), "gy")
    qkv_terms = jnp.einsum("ird,rc->idc", hidden_rows, grad_qkv, preferred_element_type=jnp.float32)
    grad_w_qkv = lax.psum_scatter(qkv_terms.astype(jnp.bfloat16), "gy")
    hidden_terms = jnp.einsum("rc,idc->ird", grad_qkv, w_qkv_full, preferred_element_type=jnp.float32)
    grad_hidden = sum_features(hidden_terms.astype(jnp.bfloat16))
    grad_hidden = grad_hidden.reshape(gy_count, seq_dev, -1)
    grad_hidden = lax.all_to_all(grad_hidden, "gy", 0, 0).transpose(1, 0, 2)
    return (grad_hidden, grad_w_qkv.astype(jnp.float32), grad_w_out.astype(jnp.float32))


def solution(mesh):
    gx_count, gy_count = mesh.shape["gx"], mesh.shape["gy"]
    images = 8 // mesh.shape["grp"]
    split_images = images == gy_count and gx_count == gy_count == 4 and mesh.shape["grp"] == 2
    body = functools.partial(image_shards, gy_count) if split_images else shards
    placed = (
        P("gy", "grp", "gx"),
        P("gy", "grp", "gx"),
        P("gy", "gx"),
        P("gy", "gx"),
        P("gy", "grp", "gx"),
        P("grp"),
    )
    return jax.shard_map(
        body,
        mesh=mesh,
        in_specs=placed,
        out_specs=(P("gy", "grp", "gx"), P(("grp", "gy"), "gx"), P(("grp", "gy"), "gx")),
        check_vma=False,
    )
```

```python
import functools
import math

import jax
import jax.numpy as jnp
from jax import lax
from jax.experimental import pallas as pl
from jax.experimental.pallas import tpu as pltpu
from jax.sharding import PartitionSpec as P

D = 3200
HEAD_DIM = 128


def contract_rows(left_rows, right_rows):
    return lax.dot_general(
        left_rows, right_rows, (((0,), (0,)), ((), ())), preferred_element_type=jnp.float32
    )


def softmax_totals(scores, valid_grid):
    masked = jnp.where(valid_grid, scores, -jnp.inf)
    row_max = jnp.max(masked, axis=3, keepdims=True)
    row_total = jnp.sum(
        jnp.where(valid_grid, jnp.exp(scores - row_max), 0.0), axis=3, keepdims=True
    )
    return row_max + jnp.log(row_total)


def shards(hidden, qkv, w_qkv, w_out, grad_out, lengths):
    seq_dev, image_count, column_count = qkv.shape
    heads_dev = column_count // (3 * HEAD_DIM)
    score_scale = 1.0 / math.sqrt(HEAD_DIM)
    row_count = seq_dev * image_count
    qkv_parts = qkv.reshape(seq_dev, image_count, heads_dev, 3, HEAD_DIM)
    query_rows = qkv_parts[:, :, :, 0]
    key_values = qkv_parts[:, :, :, 1:].reshape(seq_dev, image_count, heads_dev * 2 * HEAD_DIM)
    grad_full, hidden_full = (
        lax.all_gather(grad_out, "gx", axis=2, tiled=True),
        lax.all_gather(hidden, "gx", axis=2, tiled=True),
    )
    w_qkv_full, w_out_full, kv_full = (
        lax.all_gather(w_qkv, "gy", axis=0, tiled=True),
        lax.all_gather(w_out, "gy", axis=0, tiled=True),
        lax.all_gather(key_values, "gy", axis=0, tiled=True),
    )
    grad_rows = grad_full.reshape(row_count, D)
    grad_attn = jnp.dot(grad_rows, w_out_full, preferred_element_type=jnp.float32).astype(
        jnp.bfloat16
    )
    grad_attn = grad_attn.reshape(seq_dev, image_count, heads_dev, HEAD_DIM)
    seq_total = kv_full.shape[0]
    kv_parts = kv_full.reshape(seq_total, image_count, heads_dev, 2, HEAD_DIM)
    key_all = kv_parts[:, :, :, 0]
    value_all = kv_parts[:, :, :, 1]
    valid_all = (jnp.arange(seq_total)[None, :] < lengths[:, None])[:, None, None, :]
    scores = (
        jnp.einsum("sbhe,tbhe->bhst", query_rows, key_all, preferred_element_type=jnp.float32)
        * score_scale
    )
    log_total = softmax_totals(scores, valid_all)
    probs_full = jnp.where(valid_all, jnp.exp(scores - log_total), 0.0)
    probs_low = probs_full.astype(jnp.bfloat16)
    attn_out = jnp.einsum(
        "bhst,tbhe->sbhe", probs_low, value_all, preferred_element_type=jnp.float32
    ).astype(jnp.bfloat16)
    row_dots = jnp.sum(grad_attn.astype(jnp.float32) * attn_out.astype(jnp.float32), axis=3)
    dots_grid = row_dots.transpose(1, 2, 0)[..., None]
    grad_prob = jnp.einsum(
        "sbhe,tbhe->bhst", grad_attn, value_all, preferred_element_type=jnp.float32
    )
    grad_score = (probs_full * (grad_prob - dots_grid) * score_scale).astype(jnp.bfloat16)
    grad_q = jnp.einsum(
        "bhst,tbhe->sbhe", grad_score, key_all, preferred_element_type=jnp.float32
    ).astype(jnp.bfloat16)
    key_terms = jnp.einsum(
        "bhst,sbhe->tbhe", grad_score, query_rows, preferred_element_type=jnp.float32
    )
    value_terms = jnp.einsum(
        "bhst,sbhe->tbhe", probs_low, grad_attn, preferred_element_type=jnp.float32
    )
    kv_terms = jnp.stack([key_terms, value_terms], axis=3).reshape(
        seq_total, image_count, heads_dev * 2 * HEAD_DIM
    )
    summed = lax.psum_scatter(kv_terms, "gy", scatter_dimension=0, tiled=True)
    grad_kv = summed.astype(jnp.bfloat16).reshape(seq_dev, image_count, heads_dev, 2, HEAD_DIM)
    grad_qkv = jnp.concatenate([grad_q[:, :, :, None], grad_kv], axis=3).reshape(
        seq_dev, image_count, column_count
    )
    grad_qkv_rows = grad_qkv.reshape(row_count, column_count)
    hidden_terms = lax.dot_general(
        grad_qkv_rows, w_qkv_full, (((1,), (1,)), ((), ())), preferred_element_type=jnp.float32
    )
    grad_hidden = lax.psum_scatter(
        hidden_terms.reshape(seq_dev, image_count, D), "gx", scatter_dimension=2, tiled=True
    ).astype(jnp.bfloat16)
    attn_rows = attn_out.reshape(row_count, heads_dev * HEAD_DIM)
    out_terms = contract_rows(grad_rows, attn_rows)
    qkv_terms = contract_rows(hidden_full.reshape(row_count, D), grad_qkv_rows)
    grad_w_qkv, grad_w_out = (
        lax.psum_scatter(qkv_terms, "gy", scatter_dimension=0, tiled=True),
        lax.psum_scatter(out_terms, "gy", scatter_dimension=0, tiled=True),
    )
    return (grad_hidden, grad_w_qkv, grad_w_out)


def dot(left, right, dims):
    return lax.dot_general(left, right, ((dims[0], dims[1]), ((), ())), preferred_element_type=jnp.float32)


def head_kernel(block, length_ref, qkv_ref, grad_ref, attn_ref, dqkv_ref, key_sum, value_sum):
    seq = qkv_ref.shape[0]
    score_scale = 1.0 / math.sqrt(HEAD_DIM)
    length = length_ref[0]
    key_sum[...] = jnp.zeros_like(key_sum)
    value_sum[...] = jnp.zeros_like(value_sum)

    @pl.loop(0, seq // block)
    def _(step):
        rows = pl.ds(pl.multiple_of(step * block, block), block)
        q = qkv_ref[rows, 0:HEAD_DIM]
        k = qkv_ref[:, HEAD_DIM : 2 * HEAD_DIM]
        v = qkv_ref[:, 2 * HEAD_DIM :]
        g = grad_ref[rows, :]
        valid = lax.broadcasted_iota(jnp.int32, (1, seq), 1) < length
        scores = dot(q, k, ((1,), (1,))) * score_scale
        masked = jnp.where(valid, scores, -jnp.inf)
        row_max = jnp.max(masked, axis=1, keepdims=True)
        terms = jnp.exp(masked - row_max)
        probs = terms * (1.0 / jnp.sum(terms, axis=1, keepdims=True))
        probs_low = probs.astype(jnp.bfloat16)
        attn = dot(probs_low, v, ((1,), (0,))).astype(jnp.bfloat16)
        attn_ref[rows, :] = attn
        row_dots = jnp.sum(g.astype(jnp.float32) * attn.astype(jnp.float32), axis=1, keepdims=True)
        grad_prob = dot(g, v, ((1,), (1,)))
        grad_score = (probs * ((grad_prob - row_dots) * score_scale)).astype(jnp.bfloat16)
        dqkv_ref[rows, 0:HEAD_DIM] = dot(grad_score, k, ((1,), (0,))).astype(jnp.bfloat16)
        key_sum[...] += dot(grad_score, q, ((0,), (0,)))
        value_sum[...] += dot(probs_low, g, ((0,), (0,)))

    dqkv_ref[:, HEAD_DIM : 2 * HEAD_DIM] = key_sum[...].astype(jnp.bfloat16)
    dqkv_ref[:, 2 * HEAD_DIM :] = value_sum[...].astype(jnp.bfloat16)


def attention_backward(length, qkv, grad_attn):
    seq = qkv.shape[0]
    heads = qkv.shape[1] // (3 * HEAD_DIM)
    block = 272 if seq % 272 == 0 else seq
    return pl.pallas_call(
        functools.partial(head_kernel, block),
        grid=(heads,),
        in_specs=[
            pl.BlockSpec(memory_space=pltpu.SMEM),
            pl.BlockSpec((seq, 3 * HEAD_DIM), lambda h: (0, h)),
            pl.BlockSpec((seq, HEAD_DIM), lambda h: (0, h)),
        ],
        out_specs=[
            pl.BlockSpec((seq, HEAD_DIM), lambda h: (0, h)),
            pl.BlockSpec((seq, 3 * HEAD_DIM), lambda h: (0, h)),
        ],
        out_shape=[
            jax.ShapeDtypeStruct((seq, heads * HEAD_DIM), jnp.bfloat16),
            jax.ShapeDtypeStruct((seq, heads * 3 * HEAD_DIM), jnp.bfloat16),
        ],
        scratch_shapes=[
            pltpu.VMEM((seq, HEAD_DIM), jnp.float32),
            pltpu.VMEM((seq, HEAD_DIM), jnp.float32),
        ],
        compiler_params=pltpu.CompilerParams(vmem_limit_bytes=40 * 2**20),
        cost_estimate=pl.CostEstimate(
            flops=14 * heads * seq * seq * HEAD_DIM,
            bytes_accessed=16 * heads * seq * HEAD_DIM,
            transcendentals=heads * seq * seq,
        ),
    )(length, qkv, grad_attn)


def by_image(rows):
    swapped = lax.all_to_all(rows.transpose(1, 0, 2), "gy", 0, 0)
    return swapped.reshape(-1, rows.shape[2])


def weight_rows(weight):
    half = weight.shape[0] // 2
    group = lax.axis_index("grp")
    share = lax.dynamic_slice_in_dim(weight, group * half, half, 0)
    mine = lax.all_gather(share, "gy")
    other = lax.ppermute(mine, "grp", [(0, 1), (1, 0)])
    low = jnp.where(group == 0, mine, other)
    high = jnp.where(group == 0, other, mine)
    return jnp.concatenate([low, high], axis=1)


def spread_images(rows):
    me = lax.axis_index("gy")
    blocks = rows.transpose(1, 0, 2)
    full = jnp.zeros(blocks.shape, blocks.dtype)
    for bits in range(4):
        part = lax.dynamic_index_in_dim(blocks, me ^ bits, 0, keepdims=False)
        if bits:
            part = lax.ppermute(part, "gy", [(i, i ^ bits) for i in range(4)])
        full = lax.dynamic_update_index_in_dim(full, part, me ^ bits, 0)
    return full.reshape(-1, rows.shape[2])


def flip(value, bits):
    return lax.ppermute(value, "gx", [(i, i ^ bits) for i in range(4)])


def feature_blocks(own):
    across = flip(own, 2)
    beside = flip(own, 1)
    corner = flip(across, 1)
    me = lax.axis_index("gx")
    full = jnp.zeros((4,) + own.shape, own.dtype)
    for bits, part in enumerate((own, beside, across, corner)):
        full = lax.dynamic_update_index_in_dim(full, part, me ^ bits, 0)
    return full


def sum_features(terms):
    me = lax.axis_index("gx")

    def block(bits):
        return lax.dynamic_index_in_dim(terms, me ^ bits, 0, keepdims=False)

    far = block(2).astype(jnp.float32) + flip(block(3), 1).astype(jnp.float32)
    near = block(0).astype(jnp.float32) + flip(block(1), 1).astype(jnp.float32)
    return (near + flip(far.astype(jnp.bfloat16), 2).astype(jnp.float32)).astype(jnp.bfloat16)


def image_shards(gy_count, hidden, qkv, w_qkv, w_out, grad_out, lengths):
    image = lax.axis_index("gy")
    length = lax.dynamic_slice(lengths, (image,), (1,))
    seq_dev = qkv.shape[0]
    w_out_full = weight_rows(w_out)
    grad_own = by_image(grad_out)
    grad_rows = feature_blocks(grad_own)
    qkv, grad_own = lax.optimization_barrier((qkv, grad_own))
    qkv_rows = spread_images(qkv)
    hidden, w_qkv, qkv_rows = lax.optimization_barrier((hidden, w_qkv, qkv_rows))
    w_qkv_full = weight_rows(w_qkv)
    hidden_rows = feature_blocks(by_image(hidden))
    grad_attn = jnp.einsum(
        "ird,idc->rc", grad_rows, w_out_full, preferred_element_type=jnp.float32
    ).astype(jnp.bfloat16)
    attn_out, grad_qkv = attention_backward(length, qkv_rows, grad_attn)
    out_terms = jnp.einsum("ird,rc->idc", grad_rows, attn_out, preferred_element_type=jnp.float32)
    grad_w_out = lax.psum_scatter(out_terms.astype(jnp.bfloat16), "gy")
    qkv_terms = jnp.einsum("ird,rc->idc", hidden_rows, grad_qkv, preferred_element_type=jnp.float32)
    grad_w_qkv = lax.psum_scatter(qkv_terms.astype(jnp.bfloat16), "gy")
    hidden_terms = jnp.einsum("rc,idc->ird", grad_qkv, w_qkv_full, preferred_element_type=jnp.float32)
    grad_hidden = sum_features(hidden_terms.astype(jnp.bfloat16))
    grad_hidden = grad_hidden.reshape(gy_count, seq_dev, -1)
    grad_hidden = lax.all_to_all(grad_hidden, "gy", 0, 0).transpose(1, 0, 2)
    return (grad_hidden, grad_w_qkv.astype(jnp.float32), grad_w_out.astype(jnp.float32))


def solution(mesh):
    gx_count, gy_count = mesh.shape["gx"], mesh.shape["gy"]
    images = 8 // mesh.shape["grp"]
    split_images = images == gy_count and gx_count == gy_count == 4 and mesh.shape["grp"] == 2
    body = functools.partial(image_shards, gy_count) if split_images else shards
    placed = (
        P("gy", "grp", "gx"),
        P("gy", "grp", "gx"),
        P("gy", "gx"),
        P("gy", "gx"),
        P("gy", "grp", "gx"),
        P("grp"),
    )
    return jax.shard_map(
        body,
        mesh=mesh,
        in_specs=placed,
        out_specs=(P("gy", "grp", "gx"), P(("grp", "gy"), "gx"), P(("grp", "gy"), "gx")),
        check_vma=False,
    )
```
